512 devices in a mesh: stretch: 8 (over z_lo, core), seq: 64 (over z_hi, x, y).
Axes of the slice: x: 4, y: 8, z: 8 (z_hi: 2, z_lo: 4; z = z_hi * 4 + z_lo), core: 2. Of those that a mesh axis runs over, the one named last changes fastest.
Arguments:
- query: bfloat16 [8, 2048, 4096], P('stretch', 'seq'), may hold values from -120 to 120
- keys: bfloat16 [8, 2048, 4096], P('stretch', 'seq'), may hold values from -4 to 4
- values: bfloat16 [8, 2048, 4096], P('stretch', 'seq'), may hold values from -6 to 6
- text_keys: bfloat16 [8, 64, 128, 256], P('stretch', 'seq'), may hold values from -6 to 6
- text_values: bfloat16 [8, 64, 128, 256], P('stretch', 'seq'), may hold values from -6 to 6
- caption_len: int32 [8, 4], P('stretch'), may hold values from 1 to 128, as said below
- noise_level: int32 [8, 4], P('stretch'), may hold values from 0 to 31, as said below
- gate_table: bfloat16 [32, 4096], replicated, may hold values from 0.099609375 to 1.8984375
Outputs:
- mixed: bfloat16 [8, 2048, 4096], P('stretch', 'seq')
The draws below stay inside these ranges and needn't reach their ends.
Inputs may be any that keep to these rules, and one draw needn't show every extreme that they name: `caption_len`: some stretch of some video has all 128 caption tokens. `noise_level`: levels rise with the stretch: stretch c of every video has a level from c * (4) to (c + 1) * 4 - 1, except that stretch 8 - 1 of video 0 has level 31.
All inputs are finite; a program needn't handle non-finite values.
Results may differ from the reference program's by a relative error of at most 0.0056.
Values may be sent and summed in bfloat16 or wider, within the bound.
No kernel may reach another device: no remote copies, remote signals or barrier semaphores. Data moves between devices by JAX's collectives and lax.ppermute only.
A program may use at most 64 MiB of HBM per device.

```python
import math
import jax
import jax.numpy as jnp
from jax import lax

HEADS = 32
HD = 128
SPAN = 16
TOK_DEV = 32
TEXT = 128
LEVELS = 32
NC = 8
SAMPLES = 4
SEQ_TOK = 2048
HW = 256


def common_keys(key):
    return jnp.clip(jax.random.normal(key, (NC, SEQ_TOK, HEADS * HD), jnp.float32), -4.0, 4.0)


def draw_keys(key, part):
    return common_keys(key).astype(jnp.bfloat16)


def draw_query(key, part):
    key = jax.random.fold_in(key, 11)
    fresh = jnp.clip(jax.random.normal(key, (NC, SEQ_TOK, HEADS * HD), jnp.float32), -4.0, 4.0)
    return fresh.astype(jnp.bfloat16)


def draw_caption_len(key, part):
    key = jax.random.fold_in(key, 23)
    lengths = jax.random.randint(key, (NC, SAMPLES), 1, TEXT + 1)
    return lengths.at[0, 0].set(TEXT).astype(jnp.int32)


def draw_noise_level(key, part):
    key = jax.random.fold_in(key, 31)
    band = LEVELS // NC
    base = jnp.arange(NC, dtype=jnp.int32) * band
    offset = jax.random.randint(key, (NC, SAMPLES), 0, band)
    levels = base[:, None] + offset
    levels = levels.at[NC - 1, 0].set(LEVELS - 1)
    return levels.astype(jnp.int32)


def level_of(stream_key, extent, pieces, smallest, top_value):
    gain, own = 1.0, jax.random.fold_in(stream_key, 6)
    for position, parts in pieces:
        steps = jnp.exp(jax.random.uniform(jax.random.fold_in(own, position), (parts,), jnp.float32, smallest / len(pieces), top_value / len(pieces)))
        gain = gain * jnp.repeat(steps, extent[position] // parts).reshape([-1 if axis == position else 1 for axis in range(len(extent))])
    return gain


def centred(key, dims, width, limit, pieces=(), kind=jnp.bfloat16):
    drawn = jax.random.normal(key, dims, jnp.float32) * width
    if len(pieces) > 0:
        drawn = level_of(key, dims, pieces, -0.22, 0.18) * drawn
    return jnp.clip(drawn, min=-limit, max=limit).astype(kind)


def setup_inputs(seed: int = 0) -> dict:
    key_of = jax.random.split(jax.random.key(seed), 9)
    return {
        "query": draw_query(jax.random.fold_in(key_of[8], 71), 0),
        "keys": draw_keys(jax.random.fold_in(key_of[8], 71), 0),
        "values": centred(key_of[2], (NC, SEQ_TOK, HEADS * HD), 1.0, 6.0, ((0, 8), (1, 64))),
        "text_keys": centred(key_of[3], (NC, SAMPLES * SPAN, TEXT, HW), 1.0, 6.0, ((0, 8), (1, 64))),
        "text_values": centred(key_of[4], (NC, SAMPLES * SPAN, TEXT, HW), 1.0, 6.0, ((0, 8), (1, 64))),
        "caption_len": draw_caption_len(jax.random.fold_in(key_of[8], 71), 0),
        "noise_level": draw_noise_level(jax.random.fold_in(key_of[8], 71), 0),
        "gate_table": jnp.clip(1.0 + 0.18 * jax.random.normal(key_of[7], (LEVELS, HEADS * HD), jnp.float32), 0.099609375, 1.8984375).astype(jnp.bfloat16),
    }


def attend_one(head_query, all_keys, all_values, key_mask):
    scores = jnp.dot(head_query.astype(jnp.float32), all_keys.astype(jnp.float32).T, precision=lax.Precision.HIGHEST) * (1.0 / math.sqrt(HD))
    scores = jnp.where(key_mask[None, :], scores, -1e+30)
    row_max = lax.optimization_barrier(jnp.max(scores, axis=1, keepdims=True))
    weights = jnp.exp(scores - row_max)
    total = lax.optimization_barrier(jnp.sum(weights, axis=1, keepdims=True))
    weights_b = lax.optimization_barrier(weights.astype(jnp.bfloat16)).astype(jnp.float32)
    result = jnp.dot(weights_b, all_values.astype(jnp.float32), precision=lax.Precision.HIGHEST) / total
    return result.astype(jnp.bfloat16)

def reference(query, keys, values, text_keys, text_values, caption_len, noise_level, gate_table):
    stretch_rows = SPAN * TOK_DEV
    per_group = HEADS // SPAN
    keys_prev = jnp.concatenate([jnp.zeros_like(keys[:1]), keys[:-1]], axis=0)
    values_prev = jnp.concatenate([jnp.zeros_like(values[:1]), values[:-1]], axis=0)

    def regroup_text(table):
        shaped = table.reshape(NC, SAMPLES, SPAN, TEXT, per_group, HD).transpose(0, 1, 2, 4, 3, 5)
        return shaped.reshape(NC, SAMPLES, HEADS, TEXT, HD)
    text_k = regroup_text(text_keys)
    text_v = regroup_text(text_values)

    def per_stretch(items):
        q_c, k_c, kp_c, v_c, vp_c, tk_c, tv_c, cap_c, level_c, index = items

        def split(array):
            return array.reshape(SAMPLES, stretch_rows, HEADS, HD).transpose(0, 2, 1, 3)

        def per_sample(inner):
            q_s, k_s, kp_s, v_s, vp_s, tk_s, tv_s, cap = inner
            key_mask = jnp.concatenate([jnp.ones((stretch_rows,), bool), jnp.full((stretch_rows,), index > 0), jnp.arange(TEXT, dtype=jnp.int32) < cap])

            def per_head(head_items):
                q_h, k_h, kp_h, v_h, vp_h, tk_h, tv_h = head_items
                all_keys = jnp.concatenate([k_h, kp_h, tk_h], axis=0)
                all_values = jnp.concatenate([v_h, vp_h, tv_h], axis=0)
                return attend_one(q_h, all_keys, all_values, key_mask)
            return lax.map(per_head, (q_s, k_s, kp_s, v_s, vp_s, tk_s, tv_s))
        attended = lax.map(per_sample, (split(q_c), split(k_c), split(kp_c), split(v_c), split(vp_c), tk_c, tv_c, cap_c))
        attended = attended.transpose(0, 2, 1, 3).reshape(SAMPLES, stretch_rows, HEADS * HD)
        gate = gate_table[level_c].astype(jnp.float32)
        mixed = (gate[:, None, :] * attended.astype(jnp.float32)).astype(jnp.bfloat16)
        return mixed.reshape(SAMPLES * stretch_rows, HEADS * HD)
    return lax.map(per_stretch, (query, keys, keys_prev, values, values_prev, text_k, text_v, caption_len, noise_level, jnp.arange(NC, dtype=jnp.int32)))
```

```python
import math

import jax
import jax.numpy as jnp
from jax import lax
from jax.experimental import pallas as pl
from jax.experimental.pallas import tpu as pltpu
from jax.sharding import PartitionSpec as P

HD = 128
SPAN = 16
BLOCK_ROWS = 256
SCALE = math.log2(math.e) / math.sqrt(HD)
NT = (((1,), (1,)), ((), ()))


def attend_kernel(info_ref, q_ref, k_ref, v_ref, kp_ref, vp_ref, tk_ref, tv_ref, gate_ref, out_ref):
    rows, width = q_ref.shape
    caption = info_ref[0]
    has_prior = info_ref[1] > 0
    usable = lax.broadcasted_iota(jnp.int32, (1, tk_ref.shape[0]), 1) < caption
    for head in range(width // HD):
        cols = slice(head * HD, (head + 1) * HD)
        for block in range(rows // BLOCK_ROWS):
            span = slice(block * BLOCK_ROWS, (block + 1) * BLOCK_ROWS)
            query = q_ref[span, cols]

            def scores(keys_ref):
                return lax.dot_general(query, keys_ref[:, cols], NT, preferred_element_type=jnp.float32)

            own, prior, text = scores(k_ref), scores(kp_ref), scores(tk_ref)
            text = jnp.where(usable, text, -1e30)
            row_max = jnp.maximum(
                jnp.max(own, axis=1, keepdims=True), jnp.max(text, axis=1, keepdims=True)
            )
            with_prior = jnp.maximum(row_max, jnp.max(prior, axis=1, keepdims=True))
            row_max = jnp.where(has_prior, with_prior, row_max)
            prior_max = jnp.where(has_prior, row_max, 1e30)
            own = jnp.exp2((own - row_max) * SCALE)
            prior = jnp.exp2((prior - prior_max) * SCALE)
            text = jnp.exp2((text - row_max) * SCALE)
            total = (
                jnp.sum(own, axis=1, keepdims=True)
                + jnp.sum(prior, axis=1, keepdims=True)
                + jnp.sum(text, axis=1, keepdims=True)
            )

            def weighted(weights, values_ref):
                return jnp.dot(
                    weights.astype(jnp.bfloat16), values_ref[:, cols], preferred_element_type=jnp.float32
                )

            result = weighted(own, v_ref) + weighted(prior, vp_ref) + weighted(text, tv_ref)
            attended = (result / total).astype(jnp.bfloat16).astype(jnp.float32)
            gated = gate_ref[:, cols].astype(jnp.float32) * attended
            out_ref[span, cols] = gated.astype(jnp.bfloat16)


def attend(info, *arrays):
    vmem = pl.BlockSpec(memory_space=pltpu.VMEM)
    return pl.pallas_call(
        attend_kernel,
        out_shape=jax.ShapeDtypeStruct(arrays[0].shape, jnp.bfloat16),
        in_specs=[pl.BlockSpec(memory_space=pltpu.SMEM)] + [vmem] * len(arrays),
        out_specs=vmem,
        compiler_params=pltpu.CompilerParams(vmem_limit_bytes=32 * 1024 * 1024),
        cost_estimate=pl.CostEstimate(flops=604_000_000, bytes_accessed=2_000_000, transcendentals=1_200_000),
    )(info, *arrays)


def swap(blocks):
    videos = lax.axis_size("seq") // SPAN
    groups = [[video * SPAN + i for i in range(SPAN)] for video in range(videos)]
    return lax.all_to_all(blocks, "seq", 0, 0, axis_index_groups=groups)


def body(query, keys, values, text_keys, text_values, caption_len, noise_level, gate_table):
    tok_rows, width = query.shape[1:]
    group_width = width // SPAN
    rows = tok_rows * SPAN
    seq_index = lax.axis_index("seq")
    stretch_index = lax.axis_index("stretch")
    sample = seq_index // SPAN
    group = seq_index % SPAN

    def split(array):
        return array[0].reshape(tok_rows, SPAN, group_width).transpose(1, 0, 2)

    moved = swap(jnp.stack([split(query), split(keys), split(values)], axis=1))
    own = moved.transpose(1, 0, 2, 3).reshape(3, rows, group_width)
    last = lax.axis_size("stretch") - 1
    prior = lax.ppermute(own[1:], "stretch", [(i, i + 1) for i in range(last)])

    caption = lax.dynamic_index_in_dim(caption_len[0], sample, 0, False)
    level = lax.dynamic_index_in_dim(noise_level[0], sample, 0, False)
    info = jnp.stack([caption, stretch_index]).astype(jnp.int32)
    gate = lax.dynamic_slice(gate_table, (level, group * group_width), (1, group_width))
    mixed = attend(
        info, own[0], own[1], own[2], prior[0], prior[1], text_keys[0, 0], text_values[0, 0], gate
    )
    returned = swap(mixed.reshape(SPAN, tok_rows, group_width))
    return returned.transpose(1, 0, 2).reshape(1, tok_rows, width)


def solution(mesh):
    placed = (
        P("stretch", "seq", None),
        P("stretch", "seq", None),
        P("stretch", "seq", None),
        P("stretch", "seq", None, None),
        P("stretch", "seq", None, None),
        P("stretch", None),
        P("stretch", None),
        P(),
    )
    return jax.shard_map(
        body, mesh=mesh, in_specs=placed, out_specs=P("stretch", "seq", None), check_vma=False
    )
```

```python
import math

import jax
import jax.numpy as jnp
from jax import lax
from jax.experimental import pallas as pl
from jax.experimental.pallas import tpu as pltpu
from jax.sharding import PartitionSpec as P

HD = 128
SPAN = 16
GATE_ROWS = 16
BLOCK_ROWS = 256
SCALE = math.log2(math.e) / math.sqrt(HD)
NT = (((1,), (1,)), ((), ()))
VMEM = pl.BlockSpec(memory_space=pltpu.VMEM)
SMEM = pl.BlockSpec(memory_space=pltpu.SMEM)
HBM = pl.BlockSpec(memory_space=pltpu.HBM)
PARAMS = pltpu.CompilerParams(vmem_limit_bytes=32 * 1024 * 1024)


def split_kernel(query_ref, keys_ref, values_ref, out_ref, sems):
    rows = query_ref.shape[0]
    width = out_ref.shape[2]
    copies = []
    for part, ref in enumerate((query_ref, keys_ref, values_ref)):
        for group in range(SPAN):
            copy = pltpu.make_async_copy(
                ref.at[:, pl.ds(group * width, width)],
                out_ref.at[group, pl.ds(part * rows, rows), :],
                sems.at[part, group],
            )
            copy.start()
            copies.append(copy)
    for copy in copies:
        copy.wait()


def split(query, keys, values):
    rows, width = query.shape
    return pl.pallas_call(
        split_kernel,
        out_shape=jax.ShapeDtypeStruct((SPAN, 3 * rows, width // SPAN), query.dtype),
        in_specs=[HBM] * 3,
        out_specs=VMEM,
        scratch_shapes=[pltpu.SemaphoreType.DMA((3, SPAN))],
        compiler_params=PARAMS,
    )(*(pltpu.with_memory_space_constraint(array, pltpu.HBM) for array in (query, keys, values)))


def merge_kernel(blocks_ref, out_ref, sems):
    width = blocks_ref.shape[2]
    copies = []
    for group in range(SPAN):
        copy = pltpu.make_async_copy(
            blocks_ref.at[group], out_ref.at[:, pl.ds(group * width, width)], sems.at[group]
        )
        copy.start()
        copies.append(copy)
    for copy in copies:
        copy.wait()


def merge(blocks):
    rows, width = blocks.shape[1:]
    return pl.pallas_call(
        merge_kernel,
        out_shape=jax.ShapeDtypeStruct((rows, SPAN * width), blocks.dtype),
        in_specs=[VMEM],
        out_specs=HBM,
        scratch_shapes=[pltpu.SemaphoreType.DMA((SPAN,))],
        compiler_params=PARAMS,
    )(blocks)


def block_of(ref, block, part, rows, cols):
    count = BLOCK_ROWS // rows
    tile = ref[block * count : (block + 1) * count, part * rows : (part + 1) * rows, cols]
    return tile.reshape(BLOCK_ROWS, HD)


def whole(ref, part, rows, cols):
    return ref[:, part * rows : (part + 1) * rows, cols].reshape(ref.shape[0] * rows, HD)


def dot_keys(query, keys):
    return lax.dot_general(query, keys, NT, preferred_element_type=jnp.float32)


def dot_values(weights, values):
    return jnp.dot(weights.astype(jnp.bfloat16), values, preferred_element_type=jnp.float32)


def own_kernel(
    caption_ref, level_ref, moved_ref, text_k_ref, text_v_ref, table_ref,
    acc_ref, max_ref, total_ref, gate_ref, picked, sem,
):
    rows = moved_ref.shape[1] // 3
    width = moved_ref.shape[2]
    seq_index = lax.axis_index("seq")
    sample = seq_index // SPAN
    group = seq_index % SPAN
    level = level_ref[0, sample]
    first = pl.multiple_of(level // GATE_ROWS * GATE_ROWS, GATE_ROWS)
    start = pl.multiple_of(group * width, width)
    copy = pltpu.make_async_copy(
        table_ref.at[pl.ds(first, GATE_ROWS), pl.ds(start, width)], picked, sem
    )
    copy.start()
    usable = lax.broadcasted_iota(jnp.int32, (1, text_k_ref.shape[0]), 1) < caption_ref[0, sample]
    for head in range(width // HD):
        cols = slice(head * HD, (head + 1) * HD)
        for block in range(SPAN * rows // BLOCK_ROWS):
            span = slice(block * BLOCK_ROWS, (block + 1) * BLOCK_ROWS)
            query = block_of(moved_ref, block, 0, rows, cols)
            own = dot_keys(query, whole(moved_ref, 1, rows, cols))
            text = jnp.where(usable, dot_keys(query, text_k_ref[:, cols]), -1e30)
            row_max = jnp.maximum(
                jnp.max(own, axis=1, keepdims=True), jnp.max(text, axis=1, keepdims=True)
            )
            own = jnp.exp2((own - row_max) * SCALE)
            text = jnp.exp2((text - row_max) * SCALE)
            max_ref[head, span, :] = row_max
            total_ref[head, span, :] = jnp.sum(own, axis=1, keepdims=True) + jnp.sum(
                text, axis=1, keepdims=True
            )
            acc_ref[span, cols] = dot_values(own, whole(moved_ref, 2, rows, cols)) + dot_values(
                text, text_v_ref[:, cols]
            )
    copy.wait()
    row = lax.broadcasted_iota(jnp.int32, (GATE_ROWS, 1), 0) == level - first
    gate_ref[...] = jnp.sum(
        jnp.where(row, picked[...].astype(jnp.float32), 0.0), axis=0, keepdims=True
    )


def attend_own(caption_len, noise_level, moved, text_k, text_v, table):
    rows = moved.shape[1] // 3 * SPAN
    width = moved.shape[2]
    stat = jax.ShapeDtypeStruct((width // HD, rows, 1), jnp.float32)
    return pl.pallas_call(
        own_kernel,
        out_shape=(
            jax.ShapeDtypeStruct((rows, width), jnp.float32),
            stat,
            stat,
            jax.ShapeDtypeStruct((1, width), jnp.float32),
        ),
        in_specs=[SMEM, SMEM, VMEM, VMEM, VMEM, HBM],
        out_specs=(VMEM,) * 4,
        scratch_shapes=[
            pltpu.VMEM((GATE_ROWS, width), table.dtype),
            pltpu.SemaphoreType.DMA,
        ],
        compiler_params=PARAMS,
        cost_estimate=pl.CostEstimate(
            flops=336_000_000, bytes_accessed=1_500_000, transcendentals=655_360
        ),
    )(
        caption_len, noise_level, moved, text_k, text_v,
        pltpu.with_memory_space_constraint(table, pltpu.HBM),
    )


def prior_kernel(moved_ref, prior_ref, acc_ref, max_ref, total_ref, gate_ref, out_ref):
    rows = prior_ref.shape[1] // 2
    width = moved_ref.shape[2]
    has_prior = lax.axis_index("stretch") > 0
    for head in range(width // HD):
        cols = slice(head * HD, (head + 1) * HD)
        gate = gate_ref[:, cols]
        for block in range(SPAN * rows // BLOCK_ROWS):
            span = slice(block * BLOCK_ROWS, (block + 1) * BLOCK_ROWS)
            query = block_of(moved_ref, block, 0, rows, cols)
            prior = dot_keys(query, whole(prior_ref, 0, rows, cols))
            own_max = max_ref[head, span, :]
            row_max = jnp.maximum(own_max, jnp.max(prior, axis=1, keepdims=True))
            row_max = jnp.where(has_prior, row_max, own_max)
            shift = jnp.exp2((own_max - row_max) * SCALE)
            prior = jnp.exp2((prior - jnp.where(has_prior, row_max, 1e30)) * SCALE)
            total = total_ref[head, span, :] * shift + jnp.sum(prior, axis=1, keepdims=True)
            result = acc_ref[span, cols] * shift + dot_values(
                prior, whole(prior_ref, 1, rows, cols)
            )
            attended = (result / total).astype(jnp.bfloat16).astype(jnp.float32)
            gated = (gate * attended).astype(out_ref.dtype)
            count = BLOCK_ROWS // rows
            out_ref[block * count : (block + 1) * count, :, cols] = gated.reshape(count, rows, HD)


def attend_prior(moved, prior, *own):
    rows = prior.shape[1] // 2
    return pl.pallas_call(
        prior_kernel,
        out_shape=jax.ShapeDtypeStruct((SPAN, rows, moved.shape[2]), jnp.bfloat16),
        in_specs=[VMEM] * (2 + len(own)),
        out_specs=VMEM,
        compiler_params=PARAMS,
        cost_estimate=pl.CostEstimate(
            flops=268_000_000, bytes_accessed=2_000_000, transcendentals=524_288
        ),
    )(moved, prior, *own)


def swap(blocks):
    videos = lax.axis_size("seq") // SPAN
    groups = [[video * SPAN + i for i in range(SPAN)] for video in range(videos)]
    return lax.all_to_all(blocks, "seq", 0, 0, axis_index_groups=groups)


def body(query, keys, values, text_keys, text_values, caption_len, noise_level, gate_table):
    tok_rows = query.shape[1]
    moved = swap(split(query[0], keys[0], values[0]))
    last = lax.axis_size("stretch") - 1
    prior = lax.ppermute(moved[:, tok_rows:], "stretch", [(i, i + 1) for i in range(last)])
    own = attend_own(
        caption_len, noise_level, moved, text_keys[0, 0], text_values[0, 0], gate_table
    )
    mixed = attend_prior(moved, prior, *own)
    return merge(swap(mixed))[None]


def solution(mesh):
    placed = (
        P("stretch", "seq", None),
        P("stretch", "seq", None),
        P("stretch", "seq", None),
        P("stretch", "seq", None, None),
        P("stretch", "seq", None, None),
        P("stretch", None),
        P("stretch", None),
        P(),
    )
    return jax.shard_map(
        body, mesh=mesh, in_specs=placed, out_specs=P("stretch", "seq", None), check_vma=False
    )
```

```python
import math

import jax
import jax.numpy as jnp
from jax import lax
from jax.experimental import pallas as pl
from jax.experimental.pallas import tpu as pltpu
from jax.sharding import PartitionSpec as P

HD = 128
SPAN = 16
GATE_ROWS = 16
TILE_ROWS = 8
BLOCK_ROWS = 256
SCALE = math.log2(math.e) / math.sqrt(HD)
NT = (((1,), (1,)), ((), ()))
VMEM = pl.BlockSpec(memory_space=pltpu.VMEM)
SMEM = pl.BlockSpec(memory_space=pltpu.SMEM)
HBM = pl.BlockSpec(memory_space=pltpu.HBM)
PARAMS = pltpu.CompilerParams(vmem_limit_bytes=32 * 1024 * 1024)


def tiles_of(array):
    rows, width = array.shape
    view = array.reshape(rows // TILE_ROWS, TILE_ROWS, SPAN, width // SPAN // HD, HD)
    return view.transpose(0, 2, 3, 1, 4)


def rows_of(tiles):
    lead = tiles.shape[:-4]
    strips, across, tile_rows, tile_cols = tiles.shape[-4:]
    view = jnp.swapaxes(tiles, -3, -2)
    return view.reshape(*lead, strips * tile_rows, across * tile_cols)


def split_kernel(query_ref, keys_ref, values_ref, out_ref, sems):
    copies = []
    for part, ref in enumerate((query_ref, keys_ref, values_ref)):
        for strip in range(ref.shape[0]):
            copy = pltpu.make_async_copy(
                ref.at[strip], out_ref.at[:, part, strip], sems.at[part, strip]
            )
            copy.start()
            copies.append(copy)
    for copy in copies:
        copy.wait()


def split(*arrays):
    tiles = [pltpu.with_memory_space_constraint(tiles_of(array), pltpu.HBM) for array in arrays]
    strips, groups, *tile = tiles[0].shape
    return pl.pallas_call(
        split_kernel,
        out_shape=jax.ShapeDtypeStruct((groups, len(tiles), strips, *tile), tiles[0].dtype),
        in_specs=[HBM] * len(tiles),
        out_specs=VMEM,
        scratch_shapes=[pltpu.SemaphoreType.DMA((len(tiles), strips))],
        compiler_params=PARAMS,
    )(*tiles)


def merge_kernel(blocks_ref, out_ref, sems):
    copies = []
    for strip in range(out_ref.shape[0]):
        copy = pltpu.make_async_copy(blocks_ref.at[:, strip], out_ref.at[strip], sems.at[strip])
        copy.start()
        copies.append(copy)
    for copy in copies:
        copy.wait()


def merge(blocks):
    groups, rows, width = blocks.shape
    view = blocks.reshape(groups, rows // TILE_ROWS, TILE_ROWS, width // HD, HD)
    view = view.transpose(0, 1, 3, 2, 4)
    strips = view.shape[1]
    out = pl.pallas_call(
        merge_kernel,
        out_shape=jax.ShapeDtypeStruct((strips, groups, *view.shape[2:]), blocks.dtype),
        in_specs=[VMEM],
        out_specs=HBM,
        scratch_shapes=[pltpu.SemaphoreType.DMA((strips,))],
        compiler_params=PARAMS,
    )(view)
    return out.transpose(0, 3, 1, 2, 4).reshape(rows, groups * width)


def pick_kernel(caption_ref, level_ref, table_ref, gate_ref, bias_ref, picked, sem):
    width = gate_ref.shape[1]
    seq_index = lax.axis_index("seq")
    sample = seq_index // SPAN
    level = level_ref[0, sample]
    first = pl.multiple_of(level // GATE_ROWS * GATE_ROWS, GATE_ROWS)
    start = pl.multiple_of(seq_index % SPAN * width, width)
    copy = pltpu.make_async_copy(
        table_ref.at[pl.ds(first, GATE_ROWS), pl.ds(start, width)], picked, sem
    )
    copy.start()
    slot = lax.broadcasted_iota(jnp.int32, bias_ref.shape, 1)
    bias_ref[...] = jnp.where(slot < caption_ref[0, sample], 0.0, -1e30)
    copy.wait()
    row = lax.broadcasted_iota(jnp.int32, (GATE_ROWS, 1), 0) == level - first
    gate_ref[...] = jnp.sum(
        jnp.where(row, picked[...].astype(jnp.float32), 0.0), axis=0, keepdims=True
    )


def pick(caption_len, noise_level, table, slots):
    width = table.shape[1] // SPAN
    return pl.pallas_call(
        pick_kernel,
        out_shape=(
            jax.ShapeDtypeStruct((1, width), jnp.float32),
            jax.ShapeDtypeStruct((1, slots), jnp.float32),
        ),
        in_specs=[SMEM, SMEM, HBM],
        out_specs=(VMEM, VMEM),
        scratch_shapes=[pltpu.VMEM((GATE_ROWS, width), table.dtype), pltpu.SemaphoreType.DMA],
        compiler_params=PARAMS,
    )(caption_len, noise_level, pltpu.with_memory_space_constraint(table, pltpu.HBM))


def is_odd():
    return lax.axis_index("stretch") % 2 == 1


def block_of(ref, block, part, rows, cols):
    count = BLOCK_ROWS // rows
    tile = ref[block * count : (block + 1) * count, part * rows : (part + 1) * rows, cols]
    return tile.reshape(BLOCK_ROWS, HD)


def whole(ref, part, rows, cols):
    return ref[:, part * rows : (part + 1) * rows, cols].reshape(ref.shape[0] * rows, HD)


def dot_keys(query, keys):
    return lax.dot_general(query, keys, NT, preferred_element_type=jnp.float32)


def dot_values(weights, values):
    return jnp.dot(weights.astype(jnp.bfloat16), values, preferred_element_type=jnp.float32)


def row_top(scores):
    return jnp.max(scores, axis=1, keepdims=True)


def row_sum(weights):
    return jnp.sum(weights, axis=1, keepdims=True)


def blocks_in(moved_ref):
    rows = moved_ref.shape[1] // 3
    for head in range(moved_ref.shape[2] // HD):
        for block in range(SPAN * rows // BLOCK_ROWS):
            span = slice(block * BLOCK_ROWS, (block + 1) * BLOCK_ROWS)
            yield head, slice(head * HD, (head + 1) * HD), block, span, rows


def store(out_ref, block, rows, cols, result, total, gate_ref):
    attended = (result / total).astype(jnp.bfloat16).astype(jnp.float32)
    gated = (gate_ref[:, cols] * attended).astype(out_ref.dtype)
    count = BLOCK_ROWS // rows
    out_ref[block * count : (block + 1) * count, :, cols] = gated.reshape(count, rows, HD)


def own_kernel(moved_ref, text_k_ref, text_v_ref, bias_ref, acc_ref, max_ref, total_ref):
    if True:
        for head, cols, block, span, rows in blocks_in(moved_ref):
            query = block_of(moved_ref, block, 0, rows, cols)
            own = dot_keys(query, whole(moved_ref, 1, rows, cols))
            text = dot_keys(query, text_k_ref[:, cols]) + bias_ref[...]
            top = jnp.maximum(row_top(own), row_top(text))
            own = jnp.exp2((own - top) * SCALE)
            text = jnp.exp2((text - top) * SCALE)
            max_ref[head, span, :] = top
            total_ref[head, span, :] = row_sum(own) + row_sum(text)
            acc_ref[span, cols] = dot_values(own, whole(moved_ref, 2, rows, cols)) + dot_values(
                text, text_v_ref[:, cols]
            )


def attend_own(moved, text_k, text_v, bias):
    rows = moved.shape[1] // 3 * SPAN
    width = moved.shape[2]
    stat = jax.ShapeDtypeStruct((width // HD, rows, 1), jnp.float32)
    return pl.pallas_call(
        own_kernel,
        out_shape=(jax.ShapeDtypeStruct((rows, width), jnp.float32), stat, stat),
        in_specs=[VMEM] * 4,
        out_specs=(VMEM,) * 3,
        compiler_params=PARAMS,
        cost_estimate=pl.CostEstimate(
            flops=336_000_000, bytes_accessed=1_500_000, transcendentals=655_360
        ),
    )(moved, text_k, text_v, bias)


def last_kernel(
    moved_ref, near_ref, far_ref, text_k_ref, text_v_ref, bias_ref, gate_ref,
    acc_ref, max_ref, total_ref, out_ref,
):
    @pl.when(is_odd())
    def _():
        add_prior(
            moved_ref, near_ref, True, acc_ref, max_ref, total_ref, gate_ref, out_ref
        )

    @pl.when(jnp.logical_not(is_odd()))
    def _():
        has_prior = lax.axis_index("stretch") > 0
        add_prior(
            moved_ref, far_ref, has_prior, acc_ref, max_ref, total_ref, gate_ref, out_ref
        )


def attend_all(
    moved_ref, prior_ref, has_prior, text_k_ref, text_v_ref, bias_ref, gate_ref, out_ref
):
    for head, cols, block, span, rows in blocks_in(moved_ref):
        query = block_of(moved_ref, block, 0, rows, cols)
        own = dot_keys(query, whole(moved_ref, 1, rows, cols))
        prior = dot_keys(query, whole(prior_ref, 0, rows, cols))
        text = dot_keys(query, text_k_ref[:, cols]) + bias_ref[...]
        top = jnp.maximum(row_top(own), row_top(text))
        top = jnp.where(has_prior, jnp.maximum(top, row_top(prior)), top)
        own = jnp.exp2((own - top) * SCALE)
        text = jnp.exp2((text - top) * SCALE)
        prior = jnp.exp2((prior - jnp.where(has_prior, top, 1e30)) * SCALE)
        total = row_sum(own) + row_sum(text) + row_sum(prior)
        result = (
            dot_values(own, whole(moved_ref, 2, rows, cols))
            + dot_values(text, text_v_ref[:, cols])
            + dot_values(prior, whole(prior_ref, 1, rows, cols))
        )
        store(out_ref, block, rows, cols, result, total, gate_ref)


def add_prior(moved_ref, prior_ref, has_prior, acc_ref, max_ref, total_ref, gate_ref, out_ref):
    for head, cols, block, span, rows in blocks_in(moved_ref):
        query = block_of(moved_ref, block, 0, rows, cols)
        prior = dot_keys(query, whole(prior_ref, 0, rows, cols))
        own_top = max_ref[head, span, :]
        top = jnp.where(has_prior, jnp.maximum(own_top, row_top(prior)), own_top)
        shift = jnp.exp2((own_top - top) * SCALE)
        prior = jnp.exp2((prior - jnp.where(has_prior, top, 1e30)) * SCALE)
        total = total_ref[head, span, :] * shift + row_sum(prior)
        result = acc_ref[span, cols] * shift + dot_values(
            prior, whole(prior_ref, 1, rows, cols)
        )
        store(out_ref, block, rows, cols, result, total, gate_ref)


def attend_last(moved, *rest):
    return pl.pallas_call(
        last_kernel,
        out_shape=jax.ShapeDtypeStruct(
            (SPAN, moved.shape[1] // 3, moved.shape[2]), jnp.bfloat16
        ),
        in_specs=[VMEM] * (1 + len(rest)),
        out_specs=VMEM,
        compiler_params=PARAMS,
        cost_estimate=pl.CostEstimate(
            flops=604_000_000, bytes_accessed=3_000_000, transcendentals=1_179_648
        ),
    )(moved, *rest)


def swap(blocks):
    videos = lax.axis_size("seq") // SPAN
    groups = [[video * SPAN + i for i in range(SPAN)] for video in range(videos)]
    return lax.all_to_all(blocks, "seq", 0, 0, axis_index_groups=groups)


def body(query, keys, values, text_keys, text_values, caption_len, noise_level, gate_table):
    tok_rows = query.shape[1]
    stretches = lax.axis_size("stretch")

    def exchanged():
        return swap(split(query[0], keys[0], values[0]))

    def shifted(blocks, first):
        route = [(i, i + 1) for i in range(first, stretches - 1, 2)]
        return lax.ppermute(blocks[:, tok_rows:], "stretch", route)

    def rows_view(tiles):
        return rows_of(tiles).reshape(SPAN, 3 * tok_rows, -1)

    odd = is_odd()
    shape = jax.eval_shape(exchanged)
    early = lax.cond(odd, exchanged, lambda: jnp.zeros(shape.shape, shape.dtype))
    far = shifted(rows_view(early), 1)
    early, caption_len, noise_level = lax.optimization_barrier((early, caption_len, noise_level))
    gate, bias = pick(caption_len, noise_level, gate_table, text_keys.shape[2])
    odd, gate, bias = lax.optimization_barrier((odd, gate, bias))
    moved = rows_view(lax.cond(odd, lambda x: x, lambda x: exchanged(), early))
    near = shifted(moved, 0)
    text = (text_keys[0, 0], text_values[0, 0], bias)
    own = attend_own(moved, *text)
    mixed = attend_last(moved, near, far, *text, gate, *own)
    return merge(swap(mixed))[None]


def solution(mesh):
    placed = (
        P("stretch", "seq", None),
        P("stretch", "seq", None),
        P("stretch", "seq", None),
        P("stretch", "seq", None, None),
        P("stretch", "seq", None, None),
        P("stretch", None),
        P("stretch", None),
        P(),
    )
    return jax.shard_map(
        body, mesh=mesh, in_specs=placed, out_specs=P("stretch", "seq", None), check_vma=False
    )
```

```python
import math

import jax
import jax.numpy as jnp
from jax import lax
from jax.experimental import pallas as pl
from jax.experimental.pallas import tpu as pltpu
from jax.sharding import PartitionSpec as P

HD = 128
SPAN = 16
GATE_ROWS = 16
TILE_ROWS = 8
SCALE = math.log2(math.e) / math.sqrt(HD)
NT = (((1,), (1,)), ((), ()))
TN = (((0,), (0,)), ((), ()))
VMEM = pl.BlockSpec(memory_space=pltpu.VMEM)
SMEM = pl.BlockSpec(memory_space=pltpu.SMEM)
HBM = pl.BlockSpec(memory_space=pltpu.HBM)
PARAMS = pltpu.CompilerParams(vmem_limit_bytes=32 * 1024 * 1024)


def tiles_of(array):
    rows, width = array.shape
    view = array.reshape(rows // TILE_ROWS, TILE_ROWS, SPAN, width // SPAN // HD, HD)
    return view.transpose(0, 2, 3, 1, 4)


def rows_of(tiles):
    lead = tiles.shape[:-4]
    strips, across, tile_rows, tile_cols = tiles.shape[-4:]
    view = jnp.swapaxes(tiles, -3, -2)
    return view.reshape(*lead, strips * tile_rows, across * tile_cols)


def split_kernel(query_ref, keys_ref, values_ref, out_ref, sems):
    copies = []
    for part, ref in enumerate((query_ref, keys_ref, values_ref)):
        for strip in range(ref.shape[0]):
            copy = pltpu.make_async_copy(
                ref.at[strip], out_ref.at[:, part, strip], sems.at[part, strip]
            )
            copy.start()
            copies.append(copy)
    for copy in copies:
        copy.wait()


def split(*arrays):
    tiles = [pltpu.with_memory_space_constraint(tiles_of(array), pltpu.HBM) for array in arrays]
    strips, groups, *tile = tiles[0].shape
    return pl.pallas_call(
        split_kernel,
        out_shape=jax.ShapeDtypeStruct((groups, len(tiles), strips, *tile), tiles[0].dtype),
        in_specs=[HBM] * len(tiles),
        out_specs=VMEM,
        scratch_shapes=[pltpu.SemaphoreType.DMA((len(tiles), strips))],
        compiler_params=PARAMS,
    )(*tiles)


def merge_kernel(blocks_ref, out_ref, sems):
    copies = []
    for strip in range(out_ref.shape[0]):
        copy = pltpu.make_async_copy(blocks_ref.at[:, strip], out_ref.at[strip], sems.at[strip])
        copy.start()
        copies.append(copy)
    for copy in copies:
        copy.wait()


def merge(blocks):
    groups, rows, width = blocks.shape
    view = blocks.reshape(groups, rows // TILE_ROWS, TILE_ROWS, width // HD, HD)
    view = view.transpose(0, 1, 3, 2, 4)
    strips = view.shape[1]
    out = pl.pallas_call(
        merge_kernel,
        out_shape=jax.ShapeDtypeStruct((strips, groups, *view.shape[2:]), blocks.dtype),
        in_specs=[VMEM],
        out_specs=HBM,
        scratch_shapes=[pltpu.SemaphoreType.DMA((strips,))],
        compiler_params=PARAMS,
    )(view)
    return out.transpose(0, 3, 1, 2, 4).reshape(rows, groups * width)


def pick_kernel(caption_ref, level_ref, table_ref, gate_ref, bias_ref, picked, sem):
    width = gate_ref.shape[1]
    seq_index = lax.axis_index("seq")
    sample = seq_index // SPAN
    level = level_ref[0, sample]
    first = pl.multiple_of(level // GATE_ROWS * GATE_ROWS, GATE_ROWS)
    start = pl.multiple_of(seq_index % SPAN * width, width)
    copy = pltpu.make_async_copy(
        table_ref.at[pl.ds(first, GATE_ROWS), pl.ds(start, width)], picked, sem
    )
    copy.start()
    slot = lax.broadcasted_iota(jnp.int32, bias_ref.shape, 0)
    bias_ref[...] = jnp.where(slot < caption_ref[0, sample], 0.0, -1e30)
    copy.wait()
    row = lax.broadcasted_iota(jnp.int32, (GATE_ROWS, 1), 0) == level - first
    gate_ref[...] = jnp.sum(
        jnp.where(row, picked[...].astype(jnp.float32), 0.0), axis=0, keepdims=True
    )


def pick(caption_len, noise_level, table, slots):
    width = table.shape[1] // SPAN
    return pl.pallas_call(
        pick_kernel,
        out_shape=(
            jax.ShapeDtypeStruct((1, width), jnp.float32),
            jax.ShapeDtypeStruct((slots, 1), jnp.float32),
        ),
        in_specs=[SMEM, SMEM, HBM],
        out_specs=(VMEM, VMEM),
        scratch_shapes=[pltpu.VMEM((GATE_ROWS, width), table.dtype), pltpu.SemaphoreType.DMA],
        compiler_params=PARAMS,
    )(caption_len, noise_level, pltpu.with_memory_space_constraint(table, pltpu.HBM))


def is_odd():
    return lax.axis_index("stretch") % 2 == 1


def part_of(ref, part, rows, cols):
    return ref[:, part * rows : (part + 1) * rows, cols].reshape(ref.shape[0] * rows, HD)


def scores(keys, query):
    return lax.dot_general(keys, query, NT, preferred_element_type=jnp.float32)


def weigh(weights, values):
    return lax.dot_general(
        weights.astype(jnp.bfloat16), values, TN, preferred_element_type=jnp.float32
    )


def key_top(scored):
    return jnp.max(scored, axis=0, keepdims=True)


def key_sum(weights):
    return jnp.sum(weights, axis=0, keepdims=True)


def heads_of(ref):
    return [slice(start, start + HD) for start in range(0, ref.shape[2], HD)]


def own_kernel(moved_ref, text_k_ref, text_v_ref, bias_ref, acc_ref, max_ref, total_ref):
    rows = moved_ref.shape[1] // 3
    heads = heads_of(moved_ref)
    scored = []
    for cols in heads:
        query = part_of(moved_ref, 0, rows, cols)
        own = scores(part_of(moved_ref, 1, rows, cols), query)
        scored.append((own, scores(text_k_ref[:, cols], query) + bias_ref[...]))
    weights = []
    for head, (own, text) in enumerate(scored):
        top = jnp.maximum(key_top(own), key_top(text))
        own = jnp.exp2((own - top) * SCALE)
        text = jnp.exp2((text - top) * SCALE)
        max_ref[head] = top
        total_ref[head] = key_sum(own) + key_sum(text)
        weights.append((own, text))
    for cols, (own, text) in zip(heads, weights):
        acc_ref[:, cols] = weigh(own, part_of(moved_ref, 2, rows, cols)) + weigh(
            text, text_v_ref[:, cols]
        )


def attend_own(moved, text_k, text_v, bias):
    rows = moved.shape[1] // 3 * SPAN
    width = moved.shape[2]
    stat = jax.ShapeDtypeStruct((width // HD, 1, rows), jnp.float32)
    return pl.pallas_call(
        own_kernel,
        out_shape=(jax.ShapeDtypeStruct((rows, width), jnp.float32), stat, stat),
        in_specs=[VMEM] * 4,
        out_specs=(VMEM,) * 3,
        compiler_params=PARAMS,
        cost_estimate=pl.CostEstimate(
            flops=336_000_000, bytes_accessed=1_500_000, transcendentals=655_360
        ),
    )(moved, text_k, text_v, bias)


def add_prior(moved_ref, prior_ref, has_prior, acc_ref, max_ref, total_ref, gate_ref, out_ref):
    rows = moved_ref.shape[1] // 3
    heads = heads_of(moved_ref)
    scored = [
        scores(part_of(prior_ref, 0, rows, cols), part_of(moved_ref, 0, rows, cols))
        for cols in heads
    ]
    weights = []
    for head, prior in enumerate(scored):
        own_top = max_ref[head]
        top = jnp.where(has_prior, jnp.maximum(own_top, key_top(prior)), own_top)
        shift = jnp.exp2((own_top - top) * SCALE)
        prior = jnp.exp2((prior - jnp.where(has_prior, top, 1e30)) * SCALE)
        total = total_ref[head] * shift + key_sum(prior)
        weights.append((prior, shift.reshape(-1, 1), total.reshape(-1, 1)))
    results = [
        weigh(prior, part_of(prior_ref, 1, rows, cols)) for cols, (prior, *_) in zip(heads, weights)
    ]
    for cols, result, (_, shift, total) in zip(heads, results, weights):
        attended = (acc_ref[:, cols] * shift + result) / total
        attended = attended.astype(jnp.bfloat16).astype(jnp.float32)
        gated = (gate_ref[:, cols] * attended).astype(out_ref.dtype)
        out_ref[:, :, cols] = gated.reshape(SPAN, rows, HD)


def even_kernel(moved_ref, far_ref, gate_ref, acc_ref, max_ref, total_ref, out_ref):
    @pl.when(jnp.logical_not(is_odd()))
    def _():
        has_prior = lax.axis_index("stretch") > 0
        add_prior(moved_ref, far_ref, has_prior, acc_ref, max_ref, total_ref, gate_ref, out_ref)


def odd_keys_kernel(moved_ref, keys_ref, max_ref, total_ref, weights_ref, shift_ref, sum_ref):
    @pl.when(is_odd())
    def _():
        rows = keys_ref.shape[1]
        scored = [
            scores(part_of(keys_ref, 0, rows, cols), part_of(moved_ref, 0, rows, cols))
            for cols in heads_of(keys_ref)
        ]
        for head, prior in enumerate(scored):
            own_top = max_ref[head]
            top = jnp.maximum(own_top, key_top(prior))
            shift = jnp.exp2((own_top - top) * SCALE)
            prior = jnp.exp2((prior - top) * SCALE)
            shift_ref[head] = shift
            sum_ref[head] = total_ref[head] * shift + key_sum(prior)
            weights_ref[head] = prior.astype(weights_ref.dtype)


def odd_keys(moved, keys, row_max, total):
    count, _, rows = total.shape
    stat = jax.ShapeDtypeStruct(total.shape, jnp.float32)
    return pl.pallas_call(
        odd_keys_kernel,
        out_shape=(jax.ShapeDtypeStruct((count, rows, rows), jnp.bfloat16), stat, stat),
        in_specs=[VMEM] * 4,
        out_specs=(VMEM,) * 3,
        compiler_params=PARAMS,
    )(moved, keys, row_max, total)


def odd_values_kernel(
    moved_ref, values_ref, weights_ref, acc_ref, shift_ref, sum_ref, gate_ref, even_ref, out_ref
):
    @pl.when(is_odd())
    def _():
        rows = values_ref.shape[1]
        heads = heads_of(values_ref)
        results = [
            weigh(weights_ref[head], part_of(values_ref, 0, rows, cols))
            for head, cols in enumerate(heads)
        ]
        for head, cols in enumerate(heads):
            shift, total = shift_ref[head].reshape(-1, 1), sum_ref[head].reshape(-1, 1)
            attended = (acc_ref[:, cols] * shift + results[head]) / total
            attended = attended.astype(jnp.bfloat16).astype(jnp.float32)
            gated = (gate_ref[:, cols] * attended).astype(out_ref.dtype)
            out_ref[:, :, cols] = gated.reshape(SPAN, rows, HD)

    @pl.when(jnp.logical_not(is_odd()))
    def _():
        out_ref[...] = even_ref[...]


def attend_last(kernel, *arrays, onto=None):
    moved = arrays[0]
    if onto is not None:
        arrays = (*arrays, onto)
    return pl.pallas_call(
        kernel,
        out_shape=jax.ShapeDtypeStruct(
            (SPAN, moved.shape[1] // 3, moved.shape[2]), jnp.bfloat16
        ),
        in_specs=[VMEM] * len(arrays),
        out_specs=VMEM,
        compiler_params=PARAMS,
        cost_estimate=pl.CostEstimate(
            flops=268_000_000, bytes_accessed=2_000_000, transcendentals=524_288
        ),
    )(*arrays)


def swap(blocks):
    videos = lax.axis_size("seq") // SPAN
    groups = [[video * SPAN + i for i in range(SPAN)] for video in range(videos)]
    return lax.all_to_all(blocks, "seq", 0, 0, axis_index_groups=groups)


def body(query, keys, values, text_keys, text_values, caption_len, noise_level, gate_table):
    tok_rows = query.shape[1]
    stretches = lax.axis_size("stretch")

    def exchanged():
        return swap(split(query[0], keys[0], values[0]))

    def shifted(blocks, first):
        route = [(i, i + 1) for i in range(first, stretches - 1, 2)]
        return lax.ppermute(blocks, "stretch", route)

    def rows_view(tiles):
        return rows_of(tiles).reshape(SPAN, 3 * tok_rows, -1)

    odd = is_odd()
    shape = jax.eval_shape(exchanged)
    early = lax.cond(odd, exchanged, lambda: jnp.zeros(shape.shape, shape.dtype))
    far = shifted(rows_view(early)[:, tok_rows:], 1)
    early, caption_len, noise_level = lax.optimization_barrier((early, caption_len, noise_level))
    gate, bias = pick(caption_len, noise_level, gate_table, text_keys.shape[2])
    odd, gate, bias = lax.optimization_barrier((odd, gate, bias))
    moved = rows_view(lax.cond(odd, lambda x: x, lambda x: exchanged(), early))
    near_keys = shifted(moved[:, tok_rows : 2 * tok_rows], 0)
    near_values = shifted(moved[:, 2 * tok_rows :], 0)
    text = (text_keys[0, 0], text_values[0, 0], bias)
    own = attend_own(moved, *text)
    mixed = attend_last(even_kernel, moved, far, gate, *own)
    acc, row_max, total = own
    weights, shift, total = odd_keys(moved, near_keys, row_max, total)
    mixed = attend_last(
        odd_values_kernel, moved, near_values, weights, acc, shift, total, gate, onto=mixed
    )
    return merge(swap(mixed))[None]


def solution(mesh):
    placed = (
        P("stretch", "seq", None),
        P("stretch", "seq", None),
        P("stretch", "seq", None),
        P("stretch", "seq", None, None),
        P("stretch", "seq", None, None),
        P("stretch", None),
        P("stretch", None),
        P(),
    )
    return jax.shard_map(
        body, mesh=mesh, in_specs=placed, out_specs=P("stretch", "seq", None), check_vma=False
    )
```

```python
import math

import jax
import jax.numpy as jnp
from jax import lax
from jax.experimental import pallas as pl
from jax.experimental.pallas import tpu as pltpu
from jax.sharding import PartitionSpec as P

HD = 128
SPAN = 16
GATE_ROWS = 16
TILE_ROWS = 8
SCALE = math.log2(math.e) / math.sqrt(HD)
NT = (((1,), (1,)), ((), ()))
TN = (((0,), (0,)), ((), ()))
VMEM = pl.BlockSpec(memory_space=pltpu.VMEM)
SMEM = pl.BlockSpec(memory_space=pltpu.SMEM)
HBM = pl.BlockSpec(memory_space=pltpu.HBM)
PARAMS = pltpu.CompilerParams(vmem_limit_bytes=32 * 1024 * 1024)


def tiles_of(array):
    rows, width = array.shape
    view = array.reshape(rows // TILE_ROWS, TILE_ROWS, SPAN, width // SPAN // HD, HD)
    return view.transpose(0, 2, 3, 1, 4)


def rows_of(tiles):
    lead = tiles.shape[:-4]
    strips, across, tile_rows, tile_cols = tiles.shape[-4:]
    view = jnp.swapaxes(tiles, -3, -2)
    return view.reshape(*lead, strips * tile_rows, across * tile_cols)


def split_kernel(query_ref, keys_ref, values_ref, out_ref, sems):
    copies = []
    for part, ref in enumerate((query_ref, keys_ref, values_ref)):
        for strip in range(ref.shape[0]):
            copy = pltpu.make_async_copy(
                ref.at[strip], out_ref.at[:, part, strip], sems.at[part, strip]
            )
            copy.start()
            copies.append(copy)
    for copy in copies:
        copy.wait()


def split(*arrays):
    tiles = [pltpu.with_memory_space_constraint(tiles_of(array), pltpu.HBM) for array in arrays]
    strips, groups, *tile = tiles[0].shape
    return pl.pallas_call(
        split_kernel,
        out_shape=jax.ShapeDtypeStruct((groups, len(tiles), strips, *tile), tiles[0].dtype),
        in_specs=[HBM] * len(tiles),
        out_specs=VMEM,
        scratch_shapes=[pltpu.SemaphoreType.DMA((len(tiles), strips))],
        compiler_params=PARAMS,
    )(*tiles)


def merge_kernel(blocks_ref, out_ref, sems):
    copies = []
    for strip in range(out_ref.shape[0]):
        copy = pltpu.make_async_copy(blocks_ref.at[:, strip], out_ref.at[strip], sems.at[strip])
        copy.start()
        copies.append(copy)
    for copy in copies:
        copy.wait()


def merge(blocks):
    groups, rows, width = blocks.shape
    view = blocks.reshape(groups, rows // TILE_ROWS, TILE_ROWS, width // HD, HD)
    view = view.transpose(0, 1, 3, 2, 4)
    strips = view.shape[1]
    out = pl.pallas_call(
        merge_kernel,
        out_shape=jax.ShapeDtypeStruct((strips, groups, *view.shape[2:]), blocks.dtype),
        in_specs=[VMEM],
        out_specs=HBM,
        scratch_shapes=[pltpu.SemaphoreType.DMA((strips,))],
        compiler_params=PARAMS,
    )(view)
    return out.transpose(0, 3, 1, 2, 4).reshape(rows, groups * width)


def pick_kernel(
    caption_ref, level_ref, table_ref, text_k_hbm, text_v_hbm,
    gate_ref, bias_ref, text_k_ref, text_v_ref, picked, sems,
):
    width = gate_ref.shape[1]
    seq_index = lax.axis_index("seq")
    sample = seq_index // SPAN
    level = level_ref[0, sample]
    first = pl.multiple_of(level // GATE_ROWS * GATE_ROWS, GATE_ROWS)
    start = pl.multiple_of(seq_index % SPAN * width, width)
    copies = [
        pltpu.make_async_copy(
            table_ref.at[pl.ds(first, GATE_ROWS), pl.ds(start, width)], picked, sems.at[0]
        ),
        pltpu.make_async_copy(text_k_hbm, text_k_ref, sems.at[1]),
        pltpu.make_async_copy(text_v_hbm, text_v_ref, sems.at[2]),
    ]
    for copy in copies:
        copy.start()
    slot = lax.broadcasted_iota(jnp.int32, bias_ref.shape, 0)
    bias_ref[...] = jnp.where(slot < caption_ref[0, sample], 0.0, -1e30)
    for copy in copies:
        copy.wait()
    row = lax.broadcasted_iota(jnp.int32, (GATE_ROWS, 1), 0) == level - first
    gate_ref[...] = jnp.sum(
        jnp.where(row, picked[...].astype(jnp.float32), 0.0), axis=0, keepdims=True
    )


def pick(caption_len, noise_level, *arrays):
    table, text_k, text_v = arrays
    width = table.shape[1] // SPAN
    return pl.pallas_call(
        pick_kernel,
        out_shape=(
            jax.ShapeDtypeStruct((1, width), jnp.float32),
            jax.ShapeDtypeStruct((text_k.shape[0], 1), jnp.float32),
            jax.ShapeDtypeStruct(text_k.shape, text_k.dtype),
            jax.ShapeDtypeStruct(text_v.shape, text_v.dtype),
        ),
        in_specs=[SMEM, SMEM] + [HBM] * 3,
        out_specs=(VMEM,) * 4,
        scratch_shapes=[
            pltpu.VMEM((GATE_ROWS, width), table.dtype),
            pltpu.SemaphoreType.DMA((3,)),
        ],
        compiler_params=PARAMS,
    )(
        caption_len,
        noise_level,
        *(pltpu.with_memory_space_constraint(array, pltpu.HBM) for array in arrays),
    )


def is_odd():
    return lax.axis_index("stretch") % 2 == 1


def part_of(ref, part, rows, cols):
    return ref[:, part * rows : (part + 1) * rows, cols].reshape(ref.shape[0] * rows, HD)


def scores(keys, query):
    return lax.dot_general(keys, query, NT, preferred_element_type=jnp.float32)


def weigh(weights, values):
    return lax.dot_general(
        weights.astype(jnp.bfloat16), values, TN, preferred_element_type=jnp.float32
    )


def key_top(scored):
    return jnp.max(scored, axis=0, keepdims=True)


def key_sum(weights):
    return jnp.sum(weights, axis=0, keepdims=True)


def heads_of(ref):
    return [slice(start, start + HD) for start in range(0, ref.shape[2], HD)]


def own_kernel(moved_ref, text_k_ref, text_v_ref, bias_ref, acc_ref, max_ref, total_ref):
    rows = moved_ref.shape[1] // 3
    heads = heads_of(moved_ref)
    scored = []
    for cols in heads:
        query = part_of(moved_ref, 0, rows, cols)
        own = scores(part_of(moved_ref, 1, rows, cols), query)
        scored.append((own, scores(text_k_ref[:, cols], query) + bias_ref[...]))
    weights = []
    for head, (own, text) in enumerate(scored):
        top = jnp.maximum(key_top(own), key_top(text))
        own = jnp.exp2((own - top) * SCALE)
        text = jnp.exp2((text - top) * SCALE)
        max_ref[head] = top
        total_ref[head] = key_sum(own) + key_sum(text)
        weights.append((own, text))
    for cols, (own, text) in zip(heads, weights):
        acc_ref[:, cols] = weigh(own, part_of(moved_ref, 2, rows, cols)) + weigh(
            text, text_v_ref[:, cols]
        )


def attend_own(moved, text_k, text_v, bias):
    rows = moved.shape[1] // 3 * SPAN
    width = moved.shape[2]
    stat = jax.ShapeDtypeStruct((width // HD, 1, rows), jnp.float32)
    return pl.pallas_call(
        own_kernel,
        out_shape=(jax.ShapeDtypeStruct((rows, width), jnp.float32), stat, stat),
        in_specs=[VMEM] * 4,
        out_specs=(VMEM,) * 3,
        compiler_params=PARAMS,
        cost_estimate=pl.CostEstimate(
            flops=336_000_000, bytes_accessed=1_500_000, transcendentals=655_360
        ),
    )(moved, text_k, text_v, bias)


def add_prior(moved_ref, prior_ref, has_prior, acc_ref, max_ref, total_ref, gate_ref, out_ref):
    rows = moved_ref.shape[1] // 3
    heads = heads_of(moved_ref)
    scored = [
        scores(part_of(prior_ref, 0, rows, cols), part_of(moved_ref, 0, rows, cols))
        for cols in heads
    ]
    weights = []
    for head, prior in enumerate(scored):
        own_top = max_ref[head]
        top = jnp.where(has_prior, jnp.maximum(own_top, key_top(prior)), own_top)
        shift = jnp.exp2((own_top - top) * SCALE)
        prior = jnp.exp2((prior - jnp.where(has_prior, top, 1e30)) * SCALE)
        total = total_ref[head] * shift + key_sum(prior)
        weights.append((prior, shift.reshape(-1, 1), total.reshape(-1, 1)))
    results = [
        weigh(prior, part_of(prior_ref, 1, rows, cols)) for cols, (prior, *_) in zip(heads, weights)
    ]
    for cols, result, (_, shift, total) in zip(heads, results, weights):
        attended = (acc_ref[:, cols] * shift + result) / total
        attended = attended.astype(jnp.bfloat16).astype(jnp.float32)
        gated = (gate_ref[:, cols] * attended).astype(out_ref.dtype)
        out_ref[:, :, cols] = gated.reshape(SPAN, rows, HD)


def even_kernel(moved_ref, far_ref, gate_ref, acc_ref, max_ref, total_ref, out_ref):
    @pl.when(jnp.logical_not(is_odd()))
    def _():
        has_prior = lax.axis_index("stretch") > 0
        add_prior(moved_ref, far_ref, has_prior, acc_ref, max_ref, total_ref, gate_ref, out_ref)


def odd_kernel(
    moved_ref, near_ref, gate_ref, acc_ref, max_ref, total_ref, even_ref, out_ref
):
    @pl.when(is_odd())
    def _():
        add_prior(moved_ref, near_ref, True, acc_ref, max_ref, total_ref, gate_ref, out_ref)

    @pl.when(jnp.logical_not(is_odd()))
    def _():
        out_ref[...] = even_ref[...]


def attend_last(kernel, *arrays, onto=None):
    moved = arrays[0]
    if onto is not None:
        arrays = (*arrays, onto)
    return pl.pallas_call(
        kernel,
        out_shape=jax.ShapeDtypeStruct(
            (SPAN, moved.shape[1] // 3, moved.shape[2]), jnp.bfloat16
        ),
        in_specs=[VMEM] * len(arrays),
        out_specs=VMEM,
        compiler_params=PARAMS,
        cost_estimate=pl.CostEstimate(
            flops=268_000_000, bytes_accessed=2_000_000, transcendentals=524_288
        ),
    )(*arrays)


def swap(blocks):
    videos = lax.axis_size("seq") // SPAN
    groups = [[video * SPAN + i for i in range(SPAN)] for video in range(videos)]
    return lax.all_to_all(blocks, "seq", 0, 0, axis_index_groups=groups)


def body(query, keys, values, text_keys, text_values, caption_len, noise_level, gate_table):
    tok_rows = query.shape[1]
    stretches = lax.axis_size("stretch")

    def exchanged():
        return swap(split(query[0], keys[0], values[0]))

    def shifted(blocks, first):
        route = [(i, i + 1) for i in range(first, stretches - 1, 2)]
        return lax.ppermute(blocks, "stretch", route)

    def rows_view(tiles):
        return rows_of(tiles).reshape(SPAN, 3 * tok_rows, -1)

    odd = is_odd()
    shape = jax.eval_shape(exchanged)
    early = lax.cond(odd, exchanged, lambda: jnp.zeros(shape.shape, shape.dtype))
    far = shifted(rows_view(early)[:, tok_rows:], 1)
    early, caption_len, noise_level = lax.optimization_barrier((early, caption_len, noise_level))
    gate, bias, *text = pick(
        caption_len, noise_level, gate_table, text_keys[0, 0], text_values[0, 0]
    )
    odd, gate, bias, *text = lax.optimization_barrier((odd, gate, bias, *text))
    moved = rows_view(lax.cond(odd, lambda x: x, lambda x: exchanged(), early))
    near = shifted(moved[:, tok_rows:], 0)
    text = (*text, bias)
    own = attend_own(moved, *text)
    mixed = attend_last(even_kernel, moved, far, gate, *own)
    mixed = attend_last(odd_kernel, moved, near, gate, *own, onto=mixed)
    return merge(swap(mixed))[None]


def solution(mesh):
    placed = (
        P("stretch", "seq", None),
        P("stretch", "seq", None),
        P("stretch", "seq", None),
        P("stretch", "seq", None, None),
        P("stretch", "seq", None, None),
        P("stretch", None),
        P("stretch", None),
        P(),
    )
    return jax.shard_map(
        body, mesh=mesh, in_specs=placed, out_specs=P("stretch", "seq", None), check_vma=False
    )
```

```python
import math

import jax
import jax.numpy as jnp
from jax import lax
from jax.experimental import pallas as pl
from jax.experimental.pallas import tpu as pltpu
from jax.sharding import PartitionSpec as P

HD = 128
SPAN = 16
GATE_ROWS = 16
TILE_ROWS = 8
SCALE = math.log2(math.e) / math.sqrt(HD)
NT = (((1,), (1,)), ((), ()))
TN = (((0,), (0,)), ((), ()))
VMEM = pl.BlockSpec(memory_space=pltpu.VMEM)
SMEM = pl.BlockSpec(memory_space=pltpu.SMEM)
HBM = pl.BlockSpec(memory_space=pltpu.HBM)
PARAMS = pltpu.CompilerParams(vmem_limit_bytes=32 * 1024 * 1024)


def tiles_of(array):
    rows, width = array.shape
    view = array.reshape(rows // TILE_ROWS, TILE_ROWS, SPAN, width // SPAN // HD, HD)
    return view.transpose(0, 2, 3, 1, 4)


def rows_of(tiles):
    lead = tiles.shape[:-4]
    strips, across, tile_rows, tile_cols = tiles.shape[-4:]
    view = jnp.swapaxes(tiles, -3, -2)
    return view.reshape(*lead, strips * tile_rows, across * tile_cols)


def split_kernel(query_ref, keys_ref, values_ref, out_ref, sems):
    copies = []
    for part, ref in enumerate((query_ref, keys_ref, values_ref)):
        for strip in range(ref.shape[0]):
            copy = pltpu.make_async_copy(
                ref.at[strip], out_ref.at[:, part, strip], sems.at[part, strip]
            )
            copy.start()
            copies.append(copy)
    for copy in copies:
        copy.wait()


def split(*arrays):
    tiles = [pltpu.with_memory_space_constraint(tiles_of(array), pltpu.HBM) for array in arrays]
    strips, groups, *tile = tiles[0].shape
    return pl.pallas_call(
        split_kernel,
        out_shape=jax.ShapeDtypeStruct((groups, len(tiles), strips, *tile), tiles[0].dtype),
        in_specs=[HBM] * len(tiles),
        out_specs=VMEM,
        scratch_shapes=[pltpu.SemaphoreType.DMA((len(tiles), strips))],
        compiler_params=PARAMS,
    )(*tiles)


def merge_kernel(blocks_ref, out_ref, sems):
    copies = []
    for strip in range(out_ref.shape[0]):
        copy = pltpu.make_async_copy(blocks_ref.at[:, strip], out_ref.at[strip], sems.at[strip])
        copy.start()
        copies.append(copy)
    for copy in copies:
        copy.wait()


def merge(blocks):
    groups, rows, width = blocks.shape
    view = blocks.reshape(groups, rows // TILE_ROWS, TILE_ROWS, width // HD, HD)
    view = view.transpose(0, 1, 3, 2, 4)
    strips = view.shape[1]
    out = pl.pallas_call(
        merge_kernel,
        out_shape=jax.ShapeDtypeStruct((strips, groups, *view.shape[2:]), blocks.dtype),
        in_specs=[VMEM],
        out_specs=HBM,
        scratch_shapes=[pltpu.SemaphoreType.DMA((strips,))],
        compiler_params=PARAMS,
    )(view)
    return out.transpose(0, 3, 1, 2, 4).reshape(rows, groups * width)


def pick_kernel(
    caption_ref, level_ref, table_ref, text_k_hbm, text_v_hbm,
    gate_ref, bias_ref, text_k_ref, text_v_ref, picked, sems,
):
    width = picked.shape[1]
    seq_index = lax.axis_index("seq")
    sample = seq_index // SPAN
    level = level_ref[0, sample]
    first = pl.multiple_of(level // GATE_ROWS * GATE_ROWS, GATE_ROWS)
    start = pl.multiple_of(seq_index % SPAN * width, width)
    copies = [
        pltpu.make_async_copy(
            table_ref.at[pl.ds(first, GATE_ROWS), pl.ds(start, width)], picked, sems.at[0]
        ),
        pltpu.make_async_copy(text_k_hbm, text_k_ref, sems.at[1]),
        pltpu.make_async_copy(text_v_hbm, text_v_ref, sems.at[2]),
    ]
    for copy in copies:
        copy.start()
    slot = lax.broadcasted_iota(jnp.int32, bias_ref.shape, 0)
    bias_ref[...] = jnp.where(slot < caption_ref[0, sample], 0.0, -1e30)
    for copy in copies:
        copy.wait()
    row = lax.broadcasted_iota(jnp.int32, (GATE_ROWS, 1), 0) == level - first
    gate_ref[...] = jnp.sum(
        jnp.where(row, picked[...].astype(jnp.float32), 0.0), axis=0, keepdims=True
    ).reshape(width, 1)


def pick(caption_len, noise_level, *arrays):
    table, text_k, text_v = arrays
    width = table.shape[1] // SPAN
    return pl.pallas_call(
        pick_kernel,
        out_shape=(
            jax.ShapeDtypeStruct((width, 1), jnp.float32),
            jax.ShapeDtypeStruct((text_k.shape[0], 1), jnp.float32),
            jax.ShapeDtypeStruct(text_k.shape, text_k.dtype),
            jax.ShapeDtypeStruct(text_v.shape, text_v.dtype),
        ),
        in_specs=[SMEM, SMEM] + [HBM] * 3,
        out_specs=(VMEM,) * 4,
        scratch_shapes=[
            pltpu.VMEM((GATE_ROWS, width), table.dtype),
            pltpu.SemaphoreType.DMA((3,)),
        ],
        compiler_params=PARAMS,
    )(
        caption_len,
        noise_level,
        *(pltpu.with_memory_space_constraint(array, pltpu.HBM) for array in arrays),
    )


def is_odd():
    return lax.axis_index("stretch") % 2 == 1


def part_of(ref, part, rows, cols):
    return ref[:, part * rows : (part + 1) * rows, cols].reshape(ref.shape[0] * rows, HD)


def scores(keys, query):
    return lax.dot_general(keys, query, NT, preferred_element_type=jnp.float32)


def weigh(weights, values):
    return lax.dot_general(
        values, weights.astype(jnp.bfloat16), TN, preferred_element_type=jnp.float32
    )


def key_top(scored):
    return jnp.max(scored, axis=0, keepdims=True)


def key_sum(weights):
    return jnp.sum(weights, axis=0, keepdims=True)


def heads_of(ref):
    return [slice(start, start + HD) for start in range(0, ref.shape[2], HD)]


def own_kernel(moved_ref, text_k_ref, text_v_ref, bias_ref, acc_ref, max_ref, total_ref):
    rows = moved_ref.shape[1] // 3
    heads = heads_of(moved_ref)
    scored = []
    for cols in heads:
        query = part_of(moved_ref, 0, rows, cols)
        own = scores(part_of(moved_ref, 1, rows, cols), query)
        scored.append((own, scores(text_k_ref[:, cols], query) + bias_ref[...]))
    weights = []
    for head, (own, text) in enumerate(scored):
        top = jnp.maximum(key_top(own), key_top(text))
        own = jnp.exp2((own - top) * SCALE)
        text = jnp.exp2((text - top) * SCALE)
        max_ref[head] = top
        total_ref[head] = key_sum(own) + key_sum(text)
        weights.append((own, text))
    for cols, (own, text) in zip(heads, weights):
        acc_ref[cols, :] = weigh(own, part_of(moved_ref, 2, rows, cols)) + weigh(
            text, text_v_ref[:, cols]
        )


def attend_own(moved, text_k, text_v, bias):
    rows = moved.shape[1] // 3 * SPAN
    width = moved.shape[2]
    stat = jax.ShapeDtypeStruct((width // HD, 1, rows), jnp.float32)
    return pl.pallas_call(
        own_kernel,
        out_shape=(jax.ShapeDtypeStruct((width, rows), jnp.float32), stat, stat),
        in_specs=[VMEM] * 4,
        out_specs=(VMEM,) * 3,
        compiler_params=PARAMS,
        cost_estimate=pl.CostEstimate(
            flops=336_000_000, bytes_accessed=1_500_000, transcendentals=655_360
        ),
    )(moved, text_k, text_v, bias)


def add_prior(moved_ref, prior_ref, has_prior, acc_ref, max_ref, total_ref, gate_ref, out_ref):
    rows = moved_ref.shape[1] // 3
    heads = heads_of(moved_ref)
    scored = [
        scores(part_of(prior_ref, 0, rows, cols), part_of(moved_ref, 0, rows, cols))
        for cols in heads
    ]
    weights = []
    for head, prior in enumerate(scored):
        own_top = max_ref[head]
        top = jnp.where(has_prior, jnp.maximum(own_top, key_top(prior)), own_top)
        shift = jnp.exp2((own_top - top) * SCALE)
        prior = jnp.exp2((prior - jnp.where(has_prior, top, 1e30)) * SCALE)
        total = total_ref[head] * shift + key_sum(prior)
        weights.append((prior, shift, 1.0 / total))
    results = [
        weigh(prior, part_of(prior_ref, 1, rows, cols)) for cols, (prior, *_) in zip(heads, weights)
    ]
    for cols, result, (_, shift, inverse) in zip(heads, results, weights):
        attended = (acc_ref[cols, :] * shift + result) * inverse
        attended = attended.astype(jnp.bfloat16).astype(jnp.float32)
        gated = (gate_ref[cols, :] * attended).astype(out_ref.dtype)
        out_ref[:, :, cols] = gated.T.reshape(SPAN, rows, HD)


def even_kernel(moved_ref, far_ref, gate_ref, acc_ref, max_ref, total_ref, out_ref):
    @pl.when(jnp.logical_not(is_odd()))
    def _():
        has_prior = lax.axis_index("stretch") > 0
        add_prior(moved_ref, far_ref, has_prior, acc_ref, max_ref, total_ref, gate_ref, out_ref)


def odd_kernel(
    moved_ref, near_ref, gate_ref, acc_ref, max_ref, total_ref, even_ref, out_ref
):
    @pl.when(is_odd())
    def _():
        add_prior(moved_ref, near_ref, True, acc_ref, max_ref, total_ref, gate_ref, out_ref)

    @pl.when(jnp.logical_not(is_odd()))
    def _():
        out_ref[...] = even_ref[...]


def attend_last(kernel, *arrays, onto=None):
    moved = arrays[0]
    if onto is not None:
        arrays = (*arrays, onto)
    return pl.pallas_call(
        kernel,
        out_shape=jax.ShapeDtypeStruct(
            (SPAN, moved.shape[1] // 3, moved.shape[2]), jnp.bfloat16
        ),
        in_specs=[VMEM] * len(arrays),
        out_specs=VMEM,
        compiler_params=PARAMS,
        cost_estimate=pl.CostEstimate(
            flops=268_000_000, bytes_accessed=2_000_000, transcendentals=524_288
        ),
    )(*arrays)


def swap(blocks):
    videos = lax.axis_size("seq") // SPAN
    groups = [[video * SPAN + i for i in range(SPAN)] for video in range(videos)]
    return lax.all_to_all(blocks, "seq", 0, 0, axis_index_groups=groups)


def body(query, keys, values, text_keys, text_values, caption_len, noise_level, gate_table):
    tok_rows = query.shape[1]
    stretches = lax.axis_size("stretch")

    def exchanged():
        return swap(split(query[0], keys[0], values[0]))

    def shifted(blocks, first):
        route = [(i, i + 1) for i in range(first, stretches - 1, 2)]
        return lax.ppermute(blocks, "stretch", route)

    def rows_view(tiles):
        return rows_of(tiles).reshape(SPAN, 3 * tok_rows, -1)

    odd = is_odd()
    shape = jax.eval_shape(exchanged)
    early = lax.cond(odd, exchanged, lambda: jnp.zeros(shape.shape, shape.dtype))
    far = shifted(rows_view(early)[:, tok_rows:], 1)
    early, caption_len, noise_level = lax.optimization_barrier((early, caption_len, noise_level))
    gate, bias, *text = pick(
        caption_len, noise_level, gate_table, text_keys[0, 0], text_values[0, 0]
    )
    odd, gate, bias, *text = lax.optimization_barrier((odd, gate, bias, *text))
    moved = rows_view(lax.cond(odd, lambda x: x, lambda x: exchanged(), early))
    near = shifted(moved[:, tok_rows:], 0)
    text = (*text, bias)
    own = attend_own(moved, *text)
    mixed = attend_last(even_kernel, moved, far, gate, *own)
    mixed = attend_last(odd_kernel, moved, near, gate, *own, onto=mixed)
    return merge(swap(mixed))[None]


def solution(mesh):
    placed = (
        P("stretch", "seq", None),
        P("stretch", "seq", None),
        P("stretch", "seq", None),
        P("stretch", "seq", None, None),
        P("stretch", "seq", None, None),
        P("stretch", None),
        P("stretch", None),
        P(),
    )
    return jax.shard_map(
        body, mesh=mesh, in_specs=placed, out_specs=P("stretch", "seq", None), check_vma=False
    )
```

```python
import math

import jax
import jax.numpy as jnp
from jax import lax
from jax.experimental import pallas as pl
from jax.experimental.pallas import tpu as pltpu
from jax.sharding import PartitionSpec as P

HD = 128
SPAN = 16
GATE_ROWS = 16
TILE_ROWS = 8
SCALE = math.log2(math.e) / math.sqrt(HD)
NT = (((1,), (1,)), ((), ()))
TN = (((0,), (0,)), ((), ()))
VMEM = pl.BlockSpec(memory_space=pltpu.VMEM)
SMEM = pl.BlockSpec(memory_space=pltpu.SMEM)
HBM = pl.BlockSpec(memory_space=pltpu.HBM)
PARAMS = pltpu.CompilerParams(vmem_limit_bytes=32 * 1024 * 1024)


def tiles_of(array):
    rows, width = array.shape
    view = array.reshape(rows // TILE_ROWS, TILE_ROWS, SPAN, width // SPAN // HD, HD)
    return view.transpose(0, 2, 3, 1, 4)


def rows_of(tiles):
    lead = tiles.shape[:-4]
    strips, across, tile_rows, tile_cols = tiles.shape[-4:]
    view = jnp.swapaxes(tiles, -3, -2)
    return view.reshape(*lead, strips * tile_rows, across * tile_cols)


def split_kernel(query_ref, keys_ref, values_ref, out_ref, sems):
    copies = []
    for part, ref in enumerate((query_ref, keys_ref, values_ref)):
        for strip in range(ref.shape[0]):
            copy = pltpu.make_async_copy(
                ref.at[strip], out_ref.at[:, part, strip], sems.at[part, strip]
            )
            copy.start()
            copies.append(copy)
    for copy in copies:
        copy.wait()


def split(*arrays):
    tiles = [pltpu.with_memory_space_constraint(tiles_of(array), pltpu.HBM) for array in arrays]
    strips, groups, *tile = tiles[0].shape
    return pl.pallas_call(
        split_kernel,
        out_shape=jax.ShapeDtypeStruct((groups, len(tiles), strips, *tile), tiles[0].dtype),
        in_specs=[HBM] * len(tiles),
        out_specs=VMEM,
        scratch_shapes=[pltpu.SemaphoreType.DMA((len(tiles), strips))],
        compiler_params=PARAMS,
    )(*tiles)


def merge_kernel(blocks_ref, out_ref, sems):
    copies = []
    for strip in range(out_ref.shape[0]):
        copy = pltpu.make_async_copy(blocks_ref.at[:, strip], out_ref.at[strip], sems.at[strip])
        copy.start()
        copies.append(copy)
    for copy in copies:
        copy.wait()


def merge(blocks):
    groups, rows, width = blocks.shape
    view = blocks.reshape(groups, rows // TILE_ROWS, TILE_ROWS, width // HD, HD)
    view = view.transpose(0, 1, 3, 2, 4)
    strips = view.shape[1]
    out = pl.pallas_call(
        merge_kernel,
        out_shape=jax.ShapeDtypeStruct((strips, groups, *view.shape[2:]), blocks.dtype),
        in_specs=[VMEM],
        out_specs=HBM,
        scratch_shapes=[pltpu.SemaphoreType.DMA((strips,))],
        compiler_params=PARAMS,
    )(view)
    return out.transpose(0, 3, 1, 2, 4).reshape(rows, groups * width)


def pick_kernel(
    caption_ref, level_ref, table_ref, text_k_hbm, text_v_hbm,
    gate_ref, bias_ref, text_k_ref, text_v_ref, picked, sems,
):
    width = picked.shape[1]
    seq_index = lax.axis_index("seq")
    sample = seq_index // SPAN
    level = level_ref[0, sample]
    first = pl.multiple_of(level // GATE_ROWS * GATE_ROWS, GATE_ROWS)
    start = pl.multiple_of(seq_index % SPAN * width, width)
    copies = [
        pltpu.make_async_copy(
            table_ref.at[pl.ds(first, GATE_ROWS), pl.ds(start, width)], picked, sems.at[0]
        ),
        pltpu.make_async_copy(text_k_hbm, text_k_ref, sems.at[1]),
        pltpu.make_async_copy(text_v_hbm, text_v_ref, sems.at[2]),
    ]
    for copy in copies:
        copy.start()
    slot = lax.broadcasted_iota(jnp.int32, bias_ref.shape, 0)
    bias_ref[...] = jnp.where(slot < caption_ref[0, sample], 0.0, -1e30)
    for copy in copies:
        copy.wait()
    row = lax.broadcasted_iota(jnp.int32, (GATE_ROWS, 1), 0) == level - first
    gate_ref[...] = jnp.sum(
        jnp.where(row, picked[...].astype(jnp.float32), 0.0), axis=0, keepdims=True
    ).reshape(width, 1)


def pick(caption_len, noise_level, *arrays):
    table, text_k, text_v = arrays
    width = table.shape[1] // SPAN
    return pl.pallas_call(
        pick_kernel,
        out_shape=(
            jax.ShapeDtypeStruct((width, 1), jnp.float32),
            jax.ShapeDtypeStruct((text_k.shape[0], 1), jnp.float32),
            jax.ShapeDtypeStruct(text_k.shape, text_k.dtype),
            jax.ShapeDtypeStruct(text_v.shape, text_v.dtype),
        ),
        in_specs=[SMEM, SMEM] + [HBM] * 3,
        out_specs=(VMEM,) * 4,
        scratch_shapes=[
            pltpu.VMEM((GATE_ROWS, width), table.dtype),
            pltpu.SemaphoreType.DMA((3,)),
        ],
        compiler_params=PARAMS,
    )(
        caption_len,
        noise_level,
        *(pltpu.with_memory_space_constraint(array, pltpu.HBM) for array in arrays),
    )


def is_odd():
    return lax.axis_index("stretch") % 2 == 1


def part_of(ref, part, rows, cols):
    return ref[:, part * rows : (part + 1) * rows, cols].reshape(ref.shape[0] * rows, HD)


def scores(keys, query):
    return lax.dot_general(keys, query, NT, preferred_element_type=jnp.float32)


def weigh(weights, values):
    return lax.dot_general(
        values, weights.astype(jnp.bfloat16), TN, preferred_element_type=jnp.float32
    )


def key_top(scored):
    return jnp.max(scored, axis=0, keepdims=True)


def key_sum(weights):
    return jnp.sum(weights, axis=0, keepdims=True)


def heads_of(ref):
    return [slice(start, start + HD) for start in range(0, ref.shape[2], HD)]


def own_kernel(*refs):
    @pl.when(is_odd())
    def _():
        attend_part(*refs)


def attend_part(moved_ref, text_k_ref, text_v_ref, bias_ref, acc_ref, max_ref, total_ref):
    rows = moved_ref.shape[1] // 3
    heads = heads_of(moved_ref)
    scored = []
    for cols in heads:
        query = part_of(moved_ref, 0, rows, cols)
        own = scores(part_of(moved_ref, 1, rows, cols), query)
        scored.append((own, scores(text_k_ref[:, cols], query) + bias_ref[...]))
    weights = []
    for head, (own, text) in enumerate(scored):
        top = jnp.maximum(key_top(own), key_top(text))
        own = jnp.exp2((own - top) * SCALE)
        text = jnp.exp2((text - top) * SCALE)
        max_ref[head] = top
        total_ref[head] = key_sum(own) + key_sum(text)
        weights.append((own, text))
    for cols, (own, text) in zip(heads, weights):
        acc_ref[cols, :] = weigh(own, part_of(moved_ref, 2, rows, cols)) + weigh(
            text, text_v_ref[:, cols]
        )


def attend_own(moved, text_k, text_v, bias):
    rows = moved.shape[1] // 3 * SPAN
    width = moved.shape[2]
    stat = jax.ShapeDtypeStruct((width // HD, 1, rows), jnp.float32)
    return pl.pallas_call(
        own_kernel,
        out_shape=(jax.ShapeDtypeStruct((width, rows), jnp.float32), stat, stat),
        in_specs=[VMEM] * 4,
        out_specs=(VMEM,) * 3,
        compiler_params=PARAMS,
        cost_estimate=pl.CostEstimate(
            flops=336_000_000, bytes_accessed=1_500_000, transcendentals=655_360
        ),
    )(moved, text_k, text_v, bias)


def add_prior(moved_ref, prior_ref, has_prior, acc_ref, max_ref, total_ref, gate_ref, out_ref):
    rows = moved_ref.shape[1] // 3
    heads = heads_of(moved_ref)
    scored = [
        scores(part_of(prior_ref, 0, rows, cols), part_of(moved_ref, 0, rows, cols))
        for cols in heads
    ]
    weights = []
    for head, prior in enumerate(scored):
        own_top = max_ref[head]
        top = jnp.where(has_prior, jnp.maximum(own_top, key_top(prior)), own_top)
        shift = jnp.exp2((own_top - top) * SCALE)
        prior = jnp.exp2((prior - jnp.where(has_prior, top, 1e30)) * SCALE)
        total = total_ref[head] * shift + key_sum(prior)
        weights.append((prior, shift, 1.0 / total))
    results = [
        weigh(prior, part_of(prior_ref, 1, rows, cols)) for cols, (prior, *_) in zip(heads, weights)
    ]
    for cols, result, (_, shift, inverse) in zip(heads, results, weights):
        attended = (acc_ref[cols, :] * shift + result) * inverse
        attended = attended.astype(jnp.bfloat16).astype(jnp.float32)
        gated = (gate_ref[cols, :] * attended).astype(out_ref.dtype)
        out_ref[:, :, cols] = gated.T.reshape(SPAN, rows, HD)


def even_kernel(
    moved_ref, far_ref, text_k_ref, text_v_ref, bias_ref, gate_ref, out_ref
):
    @pl.when(jnp.logical_not(is_odd()))
    def _():
        rows = moved_ref.shape[1] // 3
        heads = heads_of(moved_ref)
        has_prior = lax.axis_index("stretch") > 0
        scored = []
        for cols in heads:
            query = part_of(moved_ref, 0, rows, cols)
            own = scores(part_of(moved_ref, 1, rows, cols), query)
            text = scores(text_k_ref[:, cols], query) + bias_ref[...]
            scored.append((own, text, scores(part_of(far_ref, 0, rows, cols), query)))
        weights = []
        for own, text, prior in scored:
            top = jnp.maximum(key_top(own), key_top(text))
            top = jnp.where(has_prior, jnp.maximum(top, key_top(prior)), top)
            own = jnp.exp2((own - top) * SCALE)
            text = jnp.exp2((text - top) * SCALE)
            prior = jnp.exp2((prior - jnp.where(has_prior, top, 1e30)) * SCALE)
            total = key_sum(own) + key_sum(text) + key_sum(prior)
            weights.append((own, text, prior, 1.0 / total))
        results = [
            weigh(own, part_of(moved_ref, 2, rows, cols))
            + weigh(text, text_v_ref[:, cols])
            + weigh(prior, part_of(far_ref, 1, rows, cols))
            for cols, (own, text, prior, _) in zip(heads, weights)
        ]
        for cols, result, (*_, inverse) in zip(heads, results, weights):
            attended = (result * inverse).astype(jnp.bfloat16).astype(jnp.float32)
            gated = (gate_ref[cols, :] * attended).astype(out_ref.dtype)
            out_ref[:, :, cols] = gated.T.reshape(SPAN, rows, HD)


def odd_kernel(
    moved_ref, near_ref, gate_ref, acc_ref, max_ref, total_ref, even_ref, out_ref
):
    @pl.when(is_odd())
    def _():
        add_prior(moved_ref, near_ref, True, acc_ref, max_ref, total_ref, gate_ref, out_ref)

    @pl.when(jnp.logical_not(is_odd()))
    def _():
        out_ref[...] = even_ref[...]


def attend_last(kernel, *arrays, onto=None):
    moved = arrays[0]
    if onto is not None:
        arrays = (*arrays, onto)
    return pl.pallas_call(
        kernel,
        out_shape=jax.ShapeDtypeStruct(
            (SPAN, moved.shape[1] // 3, moved.shape[2]), jnp.bfloat16
        ),
        in_specs=[VMEM] * len(arrays),
        out_specs=VMEM,
        compiler_params=PARAMS,
        cost_estimate=pl.CostEstimate(
            flops=268_000_000, bytes_accessed=2_000_000, transcendentals=524_288
        ),
    )(*arrays)


def swap(blocks):
    videos = lax.axis_size("seq") // SPAN
    groups = [[video * SPAN + i for i in range(SPAN)] for video in range(videos)]
    return lax.all_to_all(blocks, "seq", 0, 0, axis_index_groups=groups)


def body(query, keys, values, text_keys, text_values, caption_len, noise_level, gate_table):
    tok_rows = query.shape[1]
    stretches = lax.axis_size("stretch")

    def exchanged():
        return swap(split(query[0], keys[0], values[0]))

    def shifted(blocks, first):
        route = [(i, i + 1) for i in range(first, stretches - 1, 2)]
        return lax.ppermute(blocks, "stretch", route)

    def rows_view(tiles):
        return rows_of(tiles).reshape(SPAN, 3 * tok_rows, -1)

    odd = is_odd()
    shape = jax.eval_shape(exchanged)
    early = lax.cond(odd, exchanged, lambda: jnp.zeros(shape.shape, shape.dtype))
    far = shifted(rows_view(early)[:, tok_rows:], 1)
    early, caption_len, noise_level = lax.optimization_barrier((early, caption_len, noise_level))
    gate, bias, *text = pick(
        caption_len, noise_level, gate_table, text_keys[0, 0], text_values[0, 0]
    )
    odd, gate, bias, *text = lax.optimization_barrier((odd, gate, bias, *text))
    moved = rows_view(lax.cond(odd, lambda x: x, lambda x: exchanged(), early))
    near = shifted(moved[:, tok_rows:], 0)
    text = (*text, bias)
    own = attend_own(moved, *text)
    mixed = attend_last(even_kernel, moved, far, *text, gate)
    mixed = attend_last(odd_kernel, moved, near, gate, *own, onto=mixed)
    return merge(swap(mixed))[None]


def solution(mesh):
    placed = (
        P("stretch", "seq", None),
        P("stretch", "seq", None),
        P("stretch", "seq", None),
        P("stretch", "seq", None, None),
        P("stretch", "seq", None, None),
        P("stretch", None),
        P("stretch", None),
        P(),
    )
    return jax.shard_map(
        body, mesh=mesh, in_specs=placed, out_specs=P("stretch", "seq", None), check_vma=False
    )
```
